32 devices in a mesh: gx: 4 (over y, core), gy: 8 (over z, x).
Axes of the slice: x: 2, y: 2, z: 4, core: 2. Of those that a mesh axis runs over, the one named last changes fastest.
Arguments:
- tensor: float32 [1024, 1024, 8], P('gx', 'gy'), may hold values from -6 to 6
- sketch_one: float32 [1024, 8, 256], P('gy'), may hold values from -0.0625 to 0.0625
- sketch_two: float32 [256, 8, 256], P('gx'), may hold values from -0.125 to 0.125
Outputs:
- basis_one: float32 [1024, 256], P('gx')
- basis_two: float32 [1024, 256], P('gy')
- core: float32 [256, 256, 8], P('gx', 'gy')
The draws below stay inside these ranges and needn't reach their ends.
All inputs are finite; a program needn't handle non-finite values.
Results may differ from the reference program's by a relative error of at most 0.00008.
Values sent between devices are 32-bit elements; how exact they have to be, the bound alone decides.
A program may use at most 64 MiB of HBM per device.

```python
import jax
import jax.numpy as jnp
from jax import lax

S = 256
K3 = 8
N1 = 1024
N2 = 1024


def shard_levels(stream_key, dims, split, least, high):
    gain = 1.0
    for position, parts in split:
        steps = jax.random.uniform(jax.random.fold_in(jax.random.fold_in(stream_key, 6), position), (parts,), jnp.float32, least / len(split), high / len(split))
        gain = gain * jnp.repeat(jnp.exp(steps), dims[position] // parts).reshape((-1,) + (1,) * (len(dims) - 1 - position))
    return gain


def gaussian(rng, extent, scale, most, pieces=(), kind=jnp.bfloat16):
    factor_of = shard_levels(rng, extent, pieces, -0.22, 0.18) if pieces else 1.0
    entries = jax.random.normal(rng, extent, jnp.float32) * scale * factor_of
    return jnp.minimum(jnp.maximum(entries, -most), most).astype(kind)


def setup_inputs(seed: int = 0) -> dict:
    seeds = jax.random.split(jax.random.key(seed), 4)
    tensor = gaussian(seeds[0], (N1, N2, K3), 1.0, 6.0, ((0, 4), (1, 8)), jnp.float32)
    sketch_one = gaussian(seeds[1], (N2, K3, S), (N2 * K3) ** -0.5, 0.0625, ((0, 8),), jnp.float32)
    sketch_two = gaussian(seeds[2], (S, K3, S), (S * K3) ** -0.5, 0.125, ((0, 4),), jnp.float32)
    return dict(tensor=tensor, sketch_one=sketch_one, sketch_two=sketch_two)


def orthonormal(matrix):
    gram_total = jnp.dot(matrix.T, matrix, precision=lax.Precision.HIGHEST)
    factor = jnp.linalg.cholesky(gram_total)
    return lax.linalg.triangular_solve(factor, matrix, left_side=False, lower=True, transpose_a=True)

def reference(tensor, sketch_one, sketch_two):
    unfolded = tensor.reshape(N1, N2 * K3)
    first_sketch = jnp.dot(unfolded, sketch_one.reshape(N2 * K3, S), precision=lax.Precision.HIGHEST)
    basis_one = orthonormal(first_sketch)
    partial_core = jnp.dot(basis_one.T, unfolded, precision=lax.Precision.HIGHEST).reshape(S, N2, K3)
    second_sketch = jnp.einsum('rjk,rkc->jc', partial_core, sketch_two, precision=lax.Precision.HIGHEST)
    basis_two = orthonormal(second_sketch)
    core = jnp.einsum('rjk,js->rsk', partial_core, basis_two, precision=lax.Precision.HIGHEST)
    return (basis_one, basis_two, core)
```

```python
import functools

import jax
import jax.numpy as jnp
from jax import lax
from jax.experimental import pallas as pl
from jax.experimental.pallas import tpu as pltpu
from jax.sharding import PartitionSpec as P

HIGHEST = lax.Precision.HIGHEST
MESH = pl.DeviceIdType.MESH
BLOCK = 64
VMEM_BYTES = 40 * 1024 * 1024


def gram_local(matrix):
    return jnp.dot(matrix.T, matrix, precision=HIGHEST)


def apply_factor(gram_total, matrix):
    factor = jnp.linalg.cholesky(gram_total)
    return lax.linalg.triangular_solve(
        factor, matrix, left_side=False, lower=True, transpose_a=True
    )


def local_plain(tensor, sketch_one, sketch_two):
    rows_one, rows_two, depth = tensor.shape
    width = sketch_one.shape[2]
    unfolded = tensor.reshape(rows_one, rows_two * depth)
    partial_sketch = jnp.dot(
        unfolded, sketch_one.reshape(rows_two * depth, width), precision=HIGHEST
    )
    first_sketch = lax.psum(partial_sketch, "gy")
    gram_total = lax.psum(gram_local(first_sketch), "gx")
    basis_one = apply_factor(gram_total, first_sketch)
    rank_rows = width // lax.axis_size("gx")
    partial_core = lax.psum_scatter(
        lax.dot_general(basis_one, unfolded, (((0,), (0,)), ((), ())), precision=HIGHEST),
        "gx",
        scatter_dimension=0,
        tiled=True,
    )
    partial_core = partial_core.reshape(rank_rows, rows_two, depth)
    second_part = jnp.einsum("rjk,rkc->jc", partial_core, sketch_two, precision=HIGHEST)
    second_sketch = lax.psum(second_part, "gx")
    gram_second = lax.psum(gram_local(second_sketch), "gy")
    basis_two = apply_factor(gram_second, second_sketch)
    core_terms = jnp.einsum("rjk,js->rsk", partial_core, basis_two, precision=HIGHEST)
    core = lax.psum_scatter(core_terms, "gy", scatter_dimension=1, tiled=True)
    return (basis_one, basis_two, core)


def nn(a, b):
    return jnp.dot(a, b, precision=HIGHEST, preferred_element_type=jnp.float32)


def nt(a, b):
    return lax.dot_general(
        a, b, (((1,), (1,)), ((), ())), precision=HIGHEST, preferred_element_type=jnp.float32
    )


def tn(a, b):
    return lax.dot_general(
        a, b, (((0,), (0,)), ((), ())), precision=HIGHEST, preferred_element_type=jnp.float32
    )


def eliminate(square):
    b = square.shape[0]
    eye = (
        lax.broadcasted_iota(jnp.int32, (b, b), 0) == lax.broadcasted_iota(jnp.int32, (b, b), 1)
    ).astype(jnp.float32)
    full = jnp.concatenate([square, eye], axis=1)
    lanes = 2 * b
    groups = [full[g * 8 : g * 8 + 8] for g in range(b // 8)]
    sub = lax.broadcasted_iota(jnp.int32, (8, lanes), 0)
    for g in range(b // 8):
        later = range(g, b // 8)
        cols = []
        for j in range(8):
            lane = g * 8 + j
            cols.append(
                {h: jnp.broadcast_to(groups[h][:, lane : lane + 1], (8, lanes)) for h in later}
            )
        panel = groups[g]
        scale = jnp.zeros((8, lanes), jnp.float32)
        scaled_rows = []
        for j in range(8):
            col = cols[j]
            head = col[g]
            pivot = jnp.broadcast_to(head[j : j + 1], (8, lanes))
            inverse = 1.0 / pivot
            scale = jnp.where(sub == j, pivot, scale)
            below = jnp.where(sub > j, head, 0.0)
            row = jnp.broadcast_to(panel[j : j + 1], (8, lanes)) * inverse
            scaled_rows.append(row)
            for l in range(j + 1, 8):
                factor = jnp.broadcast_to(head[l : l + 1], (8, lanes)) * inverse
                for h in later:
                    cols[l][h] = cols[l][h] - (below if h == g else col[h]) * factor
            panel = panel - below * row
        for h in later:
            if h > g:
                value = groups[h]
                for j in range(8):
                    value = value - cols[j][h] * scaled_rows[j]
                groups[h] = value
        groups[g] = panel * lax.rsqrt(scale)
    return jnp.concatenate(groups, axis=0)[:, b:]


def factor_inverse(gram, work):
    n = gram.shape[0]
    work[:, :n] = gram
    work[:, n:] = (
        lax.broadcasted_iota(jnp.int32, (n, n), 0) == lax.broadcasted_iota(jnp.int32, (n, n), 1)
    ).astype(jnp.float32)
    for start in range(0, n, BLOCK):
        stop = start + BLOCK
        inv = eliminate(work[start:stop, start:stop])
        rows = nn(inv, work[start:stop, :])
        if stop < n:
            panel = nt(work[stop:n, start:stop], inv)
            work[stop:n, :] = work[stop:n, :] - nn(panel, rows)
        work[start:stop, n:] = rows[:, n:]


def start_copy(source, target, send_sem, recv_sem, axis, peer):
    copy = pltpu.make_async_remote_copy(
        src_ref=source,
        dst_ref=target,
        send_sem=send_sem,
        recv_sem=recv_sem,
        device_id={axis: peer},
        device_id_type=MESH,
    )
    copy.start()
    return copy


def scatter_start(source, slots, send, recv, axis, size, chunk):
    me = lax.axis_index(axis)
    copies = []
    for d in range(1, size):
        peer = lax.rem(me + d, size)
        copies.append(
            start_copy(
                chunk(source, peer), slots.at[d - 1], send.at[d - 1], recv.at[d - 1], axis, peer
            )
        )
    return copies


def gather_start(target, send, recv, axis, size, chunk):
    me = lax.axis_index(axis)
    copies = []
    for d in range(1, size):
        peer = lax.rem(me + d, size)
        mine = chunk(target, me)
        copies.append(start_copy(mine, mine, send.at[d - 1], recv.at[d - 1], axis, peer))
    return copies


def finish(copies):
    for copy in copies:
        copy.wait()


def row_chunk(rows):
    def chunk(ref, index):
        return ref.at[pl.ds(pl.multiple_of(index * rows, rows), rows)]

    return chunk


def lead_chunk(ref, index):
    return ref.at[index]


def all_reduce(ref, out, slots, send, recv, axis, size):
    me = lax.axis_index(axis)
    rows = ref.shape[0] // size
    chunk = row_chunk(rows)
    finish(scatter_start(ref, slots, send.at[0], recv.at[0], axis, size, chunk))
    mine = pl.ds(pl.multiple_of(me * rows, rows), rows)
    total = ref[mine, :]
    for d in range(size - 1):
        total = total + slots[d]
    out[mine, :] = total
    finish(gather_start(out, send.at[1], recv.at[1], axis, size, chunk))


def barrier_all(gx, gy):
    barrier = pltpu.get_barrier_semaphore()
    for axis, size in (("gx", gx), ("gy", gy)):
        me = lax.axis_index(axis)
        for d in range(1, size):
            pl.semaphore_signal(
                barrier, inc=1, device_id={axis: lax.rem(me + d, size)}, device_id_type=MESH
            )
    pl.semaphore_wait(barrier, gx + gy - 2)


def first_kernel(
    gx, gy, t_ref, s1_ref, s2_ref, y_ref, gram_ref, z_ref, s2_out,
    ypart, yfull, gpart, gfull, zall, s2_all, s2_got, yslots, gslots, zslots,
    ysend, yrecv, gsend, grecv, zsend, zrecv, ssend, srecv,
):
    depth = t_ref.shape[1]
    mine = lax.axis_index("gx")
    per = depth // gx
    for k in range(depth):
        s2_all[k // per, k % per] = s2_ref[:, k, :]
    barrier_all(gx, gy)
    moving = scatter_start(s2_all, s2_got, ssend, srecv, "gx", gx, lead_chunk)
    total = nn(t_ref[:, 0, :], s1_ref[:, 0, :])
    for k in range(1, depth):
        total = total + nn(t_ref[:, k, :], s1_ref[:, k, :])
    ypart[...] = total
    all_reduce(ypart, yfull, yslots, ysend, yrecv, "gy", gy)
    y = yfull[...]
    y_ref[...] = y
    yt = y.T
    gpart[...] = nn(yt, y)
    for k in range(depth):
        zall[k // per, k % per] = nn(yt, t_ref[:, k, :])
    zmove = scatter_start(zall, zslots, zsend, zrecv, "gx", gx, lead_chunk)
    all_reduce(gpart, gfull, gslots, gsend, grecv, "gx", gx)
    gram_ref[...] = gfull[...]
    finish(zmove)
    z = zall[mine]
    for d in range(gx - 1):
        z = z + zslots[d]
    z_ref[...] = z
    finish(moving)
    s2_out[mine] = s2_all[mine]
    for d in range(1, gx):
        s2_out[lax.rem(mine + gx - d, gx)] = s2_got[d - 1]


def second_kernel(y_ref, gram_ref, z_ref, q_ref, p_ref, work):
    n = gram_ref.shape[0]
    factor_inverse(gram_ref[...], work)
    inv = work[:, n:]
    q_ref[...] = nt(y_ref[...], inv)
    for k in range(z_ref.shape[0]):
        p_ref[k] = nn(inv, z_ref[k])


def third_kernel(
    gx, gy, p_ref, s2_ref, sketch_ref, gram_ref, w_ref,
    spart, sfull, gpart, gfull, wall, sslots, gslots, wslots,
    ssend, srecv, gsend, grecv, wsend, wrecv,
):
    per = p_ref.shape[0]
    barrier_all(gx, gy)
    rows = s2_ref.shape[2]
    total = None
    for k in range(per):
        for a in range(gx):
            term = tn(p_ref[k, a * rows : (a + 1) * rows, :], s2_ref[a, k])
            total = term if total is None else total + term
    spart[...] = total
    all_reduce(spart, sfull, sslots, ssend, srecv, "gx", gx)
    sketch = sfull[...]
    sketch_ref[...] = sketch
    gpart[...] = tn(sketch, sketch)
    part = wall.shape[2]
    for k in range(per):
        w = nn(p_ref[k], sketch)
        for g in range(gy):
            wall[g, k] = w[g * part : (g + 1) * part]
    wmove = scatter_start(wall, wslots, wsend, wrecv, "gy", gy, lead_chunk)
    all_reduce(gpart, gfull, gslots, gsend, grecv, "gy", gy)
    gram_ref[...] = gfull[...]
    finish(wmove)
    value = wall[lax.axis_index("gy")]
    for d in range(gy - 1):
        value = value + wslots[d]
    w_ref[...] = value


def fourth_kernel(sketch_ref, gram_ref, w_ref, q_ref, out_ref, work):
    n = gram_ref.shape[0]
    factor_inverse(gram_ref[...], work)
    q_ref[...] = nt(sketch_ref[...], work[:, n:])
    pieces, _, _, width = out_ref.shape
    for g in range(pieces):
        inv = work[g * width : (g + 1) * width, n:]
        for k in range(w_ref.shape[0]):
            out_ref[g, k] = nt(w_ref[k], inv)


def fifth_kernel(gx, gy, piece_ref, out_ref, got, send, recv):
    a, b = lax.axis_index("gx"), lax.axis_index("gy")
    ratio = gy // gx
    barrier = pltpu.get_barrier_semaphore()
    inside = b // ratio == a
    for sa in range(gx):
        for sb in range(ratio):
            @pl.when(jnp.logical_not(jnp.logical_and(sa == a, a * ratio + sb == b)))
            def _():
                pl.semaphore_signal(
                    barrier, inc=1, device_id={"gx": sa, "gy": a * ratio + sb}, device_id_type=MESH
                )
    pl.semaphore_wait(barrier, gy - jnp.where(inside, 1, 0))
    slot = a * ratio + lax.rem(b, ratio)

    def outgoing(g):
        return pltpu.make_async_remote_copy(
            src_ref=piece_ref.at[g],
            dst_ref=got.at[slot],
            send_sem=send.at[g],
            recv_sem=recv.at[slot],
            device_id={"gx": b // ratio, "gy": g},
            device_id_type=MESH,
        )

    for g in range(gy):
        own = jnp.logical_and(inside, g == b)

        @pl.when(jnp.logical_not(own))
        def _():
            outgoing(g).start()

    for g in range(gy):
        own = jnp.logical_and(inside, g == b)

        @pl.when(jnp.logical_not(own))
        def _():
            outgoing(g).wait_send()

    for s in range(gx * ratio):
        own = jnp.logical_and(inside, s == slot)

        @pl.when(jnp.logical_not(own))
        def _():
            pltpu.make_async_remote_copy(
                src_ref=piece_ref.at[0],
                dst_ref=got.at[s],
                send_sem=send.at[0],
                recv_sem=recv.at[s],
                device_id={"gx": b // ratio, "gy": 0},
                device_id_type=MESH,
            ).wait_recv()

            out_ref[s] = got[s]

        @pl.when(own)
        def _():
            out_ref[s] = piece_ref[b]


def call(body, outs, scratch, collective_id, *args):
    vmem = pl.BlockSpec(memory_space=pltpu.VMEM)
    if collective_id is None:
        params = pltpu.CompilerParams(vmem_limit_bytes=VMEM_BYTES)
    else:
        params = pltpu.CompilerParams(
            vmem_limit_bytes=VMEM_BYTES, collective_id=collective_id, has_side_effects=True
        )
    return pl.pallas_call(
        body,
        out_shape=[jax.ShapeDtypeStruct(shape, jnp.float32) for shape in outs],
        in_specs=[vmem] * len(args),
        out_specs=[vmem] * len(outs),
        scratch_shapes=scratch,
        compiler_params=params,
    )(*args)


def local_kernels(gx, gy, tensor, sketch_one, sketch_two):
    rows_one, rows_two, depth = tensor.shape
    width = sketch_one.shape[2]
    ranks = sketch_two.shape[0]
    per = depth // gx
    part = width // gy
    f32 = jnp.float32
    V = lambda *shape: pltpu.VMEM(shape, f32)
    D = lambda *shape: pltpu.SemaphoreType.DMA(shape)
    turned = jnp.swapaxes(tensor, 1, 2)
    y, gram, z, s2 = call(
        functools.partial(first_kernel, gx, gy),
        [(rows_one, width), (width, width), (per, width, rows_two), (gx, per, ranks, width)],
        [
            V(rows_one, width), V(rows_one, width), V(width, width), V(width, width),
            V(gx, per, width, rows_two),
            V(gx, per, ranks, width), V(gx - 1, per, ranks, width),
            V(gy - 1, rows_one // gy, width), V(gx - 1, width // gx, width),
            V(gx - 1, per, width, rows_two),
            D(2, gy - 1), D(2, gy - 1), D(2, gx - 1), D(2, gx - 1),
            D(gx - 1), D(gx - 1), D(gx - 1), D(gx - 1),
        ],
        1,
        turned, sketch_one, sketch_two,
    )
    basis_one, p = call(
        second_kernel,
        [(rows_one, width), (per, width, rows_two)],
        [V(width, 2 * width)],
        None,
        y, gram, z,
    )
    sketch, gram_second, w = call(
        functools.partial(third_kernel, gx, gy),
        [(rows_two, width), (width, width), (per, part, width)],
        [
            V(rows_two, width), V(rows_two, width), V(width, width), V(width, width),
            V(gy, per, part, width),
            V(gx - 1, rows_two // gx, width), V(gy - 1, width // gy, width),
            V(gy - 1, per, part, width),
            D(2, gx - 1), D(2, gx - 1), D(2, gy - 1), D(2, gy - 1), D(gy - 1), D(gy - 1),
        ],
        2,
        p, s2,
    )
    basis_two, pieces = call(
        fourth_kernel,
        [(rows_two, width), (gy, per, part, part)],
        [V(width, 2 * width)],
        None,
        sketch, gram_second, w,
    )
    (got,) = call(
        functools.partial(fifth_kernel, gx, gy),
        [(gy, per, part, part)],
        [V(gy, per, part, part), D(gy), D(gy)],
        3,
        pieces,
    )
    core = got.reshape(gx, gy // gx, per, part, part).transpose(1, 3, 4, 0, 2)
    core = core.reshape(ranks, part, depth)
    return basis_one, basis_two, core


def solution(mesh):
    gx, gy = mesh.shape["gx"], mesh.shape["gy"]

    def local(tensor, sketch_one, sketch_two):
        rows_one, rows_two, depth = tensor.shape
        width = sketch_one.shape[2]
        fits = (
            gx > 1
            and gy % gx == 0
            and depth % gx == 0
            and width % BLOCK == 0
            and rows_two % (8 * gx) == 0
            and rows_one % (8 * gy) == 0
            and width % (8 * gy) == 0
        )
        if fits:
            return local_kernels(gx, gy, tensor, sketch_one, sketch_two)
        return local_plain(tensor, sketch_one, sketch_two)

    in_specs = (P("gx", "gy", None), P("gy", None, None), P("gx", None, None))
    out_specs = (P("gx", None), P("gy", None), P("gx", "gy", None))
    return jax.shard_map(local, mesh=mesh, in_specs=in_specs, out_specs=out_specs, check_vma=False)
```

```python
import functools

import jax
import jax.numpy as jnp
from jax import lax
from jax.experimental import pallas as pl
from jax.experimental.pallas import tpu as pltpu
from jax.sharding import PartitionSpec as P

HIGHEST = lax.Precision.HIGHEST
MESH = pl.DeviceIdType.MESH
BLOCK = 64
VMEM_BYTES = 56 * 1024 * 1024


def gram_local(matrix):
    return jnp.dot(matrix.T, matrix, precision=HIGHEST)


def apply_factor(gram_total, matrix):
    factor = jnp.linalg.cholesky(gram_total)
    return lax.linalg.triangular_solve(
        factor, matrix, left_side=False, lower=True, transpose_a=True
    )


def local_plain(tensor, sketch_one, sketch_two):
    rows_one, rows_two, depth = tensor.shape
    width = sketch_one.shape[2]
    unfolded = tensor.reshape(rows_one, rows_two * depth)
    partial_sketch = jnp.dot(
        unfolded, sketch_one.reshape(rows_two * depth, width), precision=HIGHEST
    )
    first_sketch = lax.psum(partial_sketch, "gy")
    gram_total = lax.psum(gram_local(first_sketch), "gx")
    basis_one = apply_factor(gram_total, first_sketch)
    rank_rows = width // lax.axis_size("gx")
    partial_core = lax.psum_scatter(
        lax.dot_general(basis_one, unfolded, (((0,), (0,)), ((), ())), precision=HIGHEST),
        "gx",
        scatter_dimension=0,
        tiled=True,
    )
    partial_core = partial_core.reshape(rank_rows, rows_two, depth)
    second_part = jnp.einsum("rjk,rkc->jc", partial_core, sketch_two, precision=HIGHEST)
    second_sketch = lax.psum(second_part, "gx")
    gram_second = lax.psum(gram_local(second_sketch), "gy")
    basis_two = apply_factor(gram_second, second_sketch)
    core_terms = jnp.einsum("rjk,js->rsk", partial_core, basis_two, precision=HIGHEST)
    core = lax.psum_scatter(core_terms, "gy", scatter_dimension=1, tiled=True)
    return (basis_one, basis_two, core)


def nn(a, b):
    return jnp.dot(a, b, precision=HIGHEST, preferred_element_type=jnp.float32)


def nt(a, b):
    return lax.dot_general(
        a, b, (((1,), (1,)), ((), ())), precision=HIGHEST, preferred_element_type=jnp.float32
    )


def tn(a, b):
    return lax.dot_general(
        a, b, (((0,), (0,)), ((), ())), precision=HIGHEST, preferred_element_type=jnp.float32
    )


def eliminate(square):
    b = square.shape[0]
    eye = (
        lax.broadcasted_iota(jnp.int32, (b, b), 0) == lax.broadcasted_iota(jnp.int32, (b, b), 1)
    ).astype(jnp.float32)
    full = jnp.concatenate([square, eye], axis=1)
    lanes = 2 * b
    groups = [full[g * 8 : g * 8 + 8] for g in range(b // 8)]
    sub = lax.broadcasted_iota(jnp.int32, (8, lanes), 0)
    for g in range(b // 8):
        later = range(g, b // 8)
        cols = []
        for j in range(8):
            lane = g * 8 + j
            cols.append(
                {h: jnp.broadcast_to(groups[h][:, lane : lane + 1], (8, lanes)) for h in later}
            )
        panel = groups[g]
        scale = jnp.zeros((8, lanes), jnp.float32)
        scaled_rows = []
        for j in range(8):
            col = cols[j]
            head = col[g]
            pivot = jnp.broadcast_to(head[j : j + 1], (8, lanes))
            inverse = 1.0 / pivot
            scale = jnp.where(sub == j, pivot, scale)
            below = jnp.where(sub > j, head, 0.0)
            row = jnp.broadcast_to(panel[j : j + 1], (8, lanes)) * inverse
            scaled_rows.append(row)
            for l in range(j + 1, 8):
                factor = jnp.broadcast_to(head[l : l + 1], (8, lanes)) * inverse
                for h in later:
                    cols[l][h] = cols[l][h] - (below if h == g else col[h]) * factor
            panel = panel - below * row
        for h in later:
            if h > g:
                value = groups[h]
                for j in range(8):
                    value = value - cols[j][h] * scaled_rows[j]
                groups[h] = value
        groups[g] = panel * lax.rsqrt(scale)
    return jnp.concatenate(groups, axis=0)[:, b:]


def factor_inverse(gram, work):
    n = gram.shape[0]
    work[:, :n] = gram
    work[:, n : 2 * n] = (
        lax.broadcasted_iota(jnp.int32, (n, n), 0) == lax.broadcasted_iota(jnp.int32, (n, n), 1)
    ).astype(jnp.float32)
    for start in range(0, n, BLOCK):
        stop = start + BLOCK
        inv = eliminate(work[start:stop, start:stop])
        rows = nn(inv, work[start:stop, :])
        if stop < n:
            panel = nt(work[stop:n, start:stop], inv)
            work[stop:n, :] = work[stop:n, :] - nn(panel, rows)
        work[start:stop, n:] = rows[:, n:]


def start_copy(source, target, send_sem, recv_sem, axis, peer):
    copy = pltpu.make_async_remote_copy(
        src_ref=source,
        dst_ref=target,
        send_sem=send_sem,
        recv_sem=recv_sem,
        device_id={axis: peer},
        device_id_type=MESH,
    )
    copy.start()
    return copy


def scatter_start(source, slots, send, recv, axis, size, chunk):
    me = lax.axis_index(axis)
    copies = []
    for d in range(1, size):
        peer = lax.rem(me + d, size)
        copies.append(
            start_copy(
                chunk(source, peer), slots.at[d - 1], send.at[d - 1], recv.at[d - 1], axis, peer
            )
        )
    return copies


def gather_start(target, send, recv, axis, size, chunk):
    me = lax.axis_index(axis)
    copies = []
    for d in range(1, size):
        peer = lax.rem(me + d, size)
        mine = chunk(target, me)
        copies.append(start_copy(mine, mine, send.at[d - 1], recv.at[d - 1], axis, peer))
    return copies


def finish(copies):
    for copy in copies:
        copy.wait()


def row_chunk(rows):
    def chunk(ref, index):
        return ref.at[pl.ds(pl.multiple_of(index * rows, rows), rows)]

    return chunk


def lead_chunk(ref, index):
    return ref.at[index]


def barrier_all(gx, gy):
    a, b = lax.axis_index("gx"), lax.axis_index("gy")
    ratio = gy // gx
    barrier = pltpu.get_barrier_semaphore()
    for axis, size, me in (("gx", gx, a), ("gy", gy, b)):
        for d in range(1, size):
            pl.semaphore_signal(
                barrier, inc=1, device_id={axis: lax.rem(me + d, size)}, device_id_type=MESH
            )
    for sa in range(gx):
        for sb in range(ratio):
            @pl.when(jnp.logical_not(jnp.logical_and(sa == a, a * ratio + sb == b)))
            def _():
                pl.semaphore_signal(
                    barrier, inc=1, device_id={"gx": sa, "gy": a * ratio + sb}, device_id_type=MESH
                )
    pl.semaphore_wait(barrier, gx + gy - 2 + gy - jnp.where(b // ratio == a, 1, 0))


def sum_chunk(ref, slots, mine):
    total = ref[mine]
    for d in range(slots.shape[0]):
        total = total + slots[d]
    return total


def reduce_rows(part, out, slots, send, recv, axis, size, beside=None, after=None):
    me = lax.axis_index(axis)
    rows = part.shape[0] // size
    chunk = row_chunk(rows)
    copies = scatter_start(part, slots, send.at[0], recv.at[0], axis, size, chunk)
    if beside is not None:
        beside()
    finish(copies)
    mine = pl.ds(pl.multiple_of(me * rows, rows), rows)
    out[mine, :] = sum_chunk(part, slots, mine)
    copies = gather_start(out, send.at[1], recv.at[1], axis, size, chunk)
    if after is not None:
        after()
    finish(copies)


def exchange_pieces(gx, gy, pieces, got, out_ref, send, recv):
    a, b = lax.axis_index("gx"), lax.axis_index("gy")
    ratio = gy // gx
    inside = b // ratio == a
    slot = a * ratio + lax.rem(b, ratio)

    def outgoing(g):
        return pltpu.make_async_remote_copy(
            src_ref=pieces.at[g],
            dst_ref=got.at[slot],
            send_sem=send.at[g],
            recv_sem=recv.at[slot],
            device_id={"gx": b // ratio, "gy": g},
            device_id_type=MESH,
        )

    for g in range(gy):
        @pl.when(jnp.logical_not(jnp.logical_and(inside, g == b)))
        def _():
            outgoing(g).start()

    for s in range(gx * ratio):
        own = jnp.logical_and(inside, s == slot)

        @pl.when(jnp.logical_not(own))
        def _():
            pltpu.make_async_remote_copy(
                src_ref=pieces.at[0],
                dst_ref=got.at[s],
                send_sem=send.at[0],
                recv_sem=recv.at[s],
                device_id={"gx": b // ratio, "gy": 0},
                device_id_type=MESH,
            ).wait_recv()
            out_ref[s] = got[s]

        @pl.when(own)
        def _():
            out_ref[s] = pieces[b]

    for g in range(gy):
        @pl.when(jnp.logical_not(jnp.logical_and(inside, g == b)))
        def _():
            outgoing(g).wait_send()


def kernel(
    gx, gy, t_hbm, s1_hbm, s2_hbm, q1_ref, q2_ref, out_ref,
    t_ref, s1_ref, s2_ref, load, work,
    ypart, yfull, yslots, ysend, yrecv,
    gpart, gfull, gslots, gsend, grecv,
    zall, zslots, zsend, zrecv,
    s2_all, s2_got, s2send, s2recv,
    spart, sfull, sslots, ssend, srecv,
    hpart, hfull, hslots, hsend, hrecv,
    wall, wslots, wsend, wrecv,
    pieces, got, esend, erecv,
):
    depth = t_ref.shape[1]
    width = s1_ref.shape[2]
    a, b = lax.axis_index("gx"), lax.axis_index("gy")
    per = depth // gx
    loads = [
        pltpu.make_async_copy(src, dst, load.at[i])
        for i, (src, dst) in enumerate(((s1_hbm, s1_ref), (t_hbm, t_ref), (s2_hbm, s2_ref)))
    ]
    for copy in loads:
        copy.start()
    barrier_all(gx, gy)
    finish(loads)

    total = nn(t_ref[:, 0, :], s1_ref[:, 0, :])
    for k in range(1, depth):
        total = total + nn(t_ref[:, k, :], s1_ref[:, k, :])
    ypart[...] = total

    for_later = []

    def send_sketch():
        for k in range(depth):
            s2_all[k // per, k % per] = s2_ref[:, k, :]
        for_later.extend(scatter_start(s2_all, s2_got, s2send, s2recv, "gx", gx, lead_chunk))

    reduce_rows(ypart, yfull, yslots, ysend, yrecv, "gy", gy, beside=send_sketch)

    y = yfull[...]
    yt = y.T
    gpart[...] = nn(yt, y)
    z_moves = []

    def contract():
        for k in range(depth):
            zall[k // per, k % per] = nn(yt, t_ref[:, k, :])

    def send_contraction():
        z_moves.extend(scatter_start(zall, zslots, zsend, zrecv, "gx", gx, lead_chunk))

    reduce_rows(
        gpart, gfull, gslots, gsend, grecv, "gx", gx, beside=contract, after=send_contraction
    )
    factor_inverse(gfull[...], work)
    inv = work[:, width : 2 * width]
    q1_ref[...] = nt(yfull[...], inv)
    finish(z_moves)
    z = sum_chunk(zall, zslots, a)
    p = [nn(inv, z[k]) for k in range(per)]

    finish(for_later)
    ranks = s2_all.shape[2]
    s2_got_all = s2_all.at[a]
    total = None
    for d in range(gx):
        origin = lax.rem(a + gx - d, gx)
        for k in range(per):
            block = s2_got_all[k] if d == 0 else s2_got[d - 1, k]
            work[pl.ds(pl.multiple_of(origin * ranks, ranks), ranks), k * width : (k + 1) * width] = (
                block
            )
    for k in range(per):
        term = tn(p[k], work[:, k * width : (k + 1) * width])
        total = term if total is None else total + term
    spart[...] = total
    reduce_rows(spart, sfull, sslots, ssend, srecv, "gx", gx)

    sketch = sfull[...]
    hpart[...] = tn(sketch, sketch)
    part = wall.shape[2]
    w_moves = []

    def contract_second():
        for k in range(per):
            w = nn(p[k], sketch)
            for g in range(gy):
                wall[g, k] = w[g * part : (g + 1) * part]

    def send_second():
        w_moves.extend(scatter_start(wall, wslots, wsend, wrecv, "gy", gy, lead_chunk))

    reduce_rows(
        hpart, hfull, hslots, hsend, hrecv, "gy", gy, beside=contract_second, after=send_second
    )
    factor_inverse(hfull[...], work)
    q2_ref[...] = nt(sfull[...], work[:, width:])
    finish(w_moves)
    w = sum_chunk(wall, wslots, b)
    for g in range(gy):
        inv = work[g * part : (g + 1) * part, width:]
        for k in range(per):
            pieces[g, k] = nt(w[k], inv)
    exchange_pieces(gx, gy, pieces, got, out_ref, esend, erecv)


def local_kernels(gx, gy, tensor, sketch_one, sketch_two):
    rows_one, rows_two, depth = tensor.shape
    width = sketch_one.shape[2]
    per = depth // gx
    ranks = sketch_two.shape[0]
    part = width // gy
    f32 = jnp.float32
    V = lambda *shape: pltpu.VMEM(shape, f32)
    D = lambda *shape: pltpu.SemaphoreType.DMA(shape)

    def sums(rows, size):
        return [
            V(rows, width), V(rows, width), V(size - 1, rows // size, width),
            D(2, size - 1), D(2, size - 1),
        ]

    turned = jnp.swapaxes(tensor, 1, 2)
    vmem = pl.BlockSpec(memory_space=pltpu.VMEM)
    basis_one, basis_two, got = pl.pallas_call(
        functools.partial(kernel, gx, gy),
        out_shape=[
            jax.ShapeDtypeStruct((rows_one, width), f32),
            jax.ShapeDtypeStruct((rows_two, width), f32),
            jax.ShapeDtypeStruct((gy, per, part, part), f32),
        ],
        in_specs=[pl.BlockSpec(memory_space=pl.ANY)] * 3,
        out_specs=[vmem] * 3,
        scratch_shapes=[
            V(*turned.shape), V(*sketch_one.shape), V(*sketch_two.shape), D(3),
            V(width, max(2, per) * width),
            *sums(rows_one, gy),
            *sums(width, gx),
            V(gx, per, width, rows_two), V(gx - 1, per, width, rows_two), D(gx - 1), D(gx - 1),
            V(gx, per, ranks, width), V(gx - 1, per, ranks, width), D(gx - 1), D(gx - 1),
            *sums(rows_two, gx),
            *sums(width, gy),
            V(gy, per, part, width), V(gy - 1, per, part, width), D(gy - 1), D(gy - 1),
            V(gy, per, part, part), V(gy, per, part, part), D(gy), D(gy),
        ],
        compiler_params=pltpu.CompilerParams(
            vmem_limit_bytes=VMEM_BYTES, collective_id=1, has_side_effects=True
        ),
    )(turned, sketch_one, sketch_two)
    core = got.reshape(gx, gy // gx, per, part, part).transpose(1, 3, 4, 0, 2)
    return basis_one, basis_two, core.reshape(ranks, part, depth)


def solution(mesh):
    gx, gy = mesh.shape["gx"], mesh.shape["gy"]

    def local(tensor, sketch_one, sketch_two):
        rows_one, rows_two, depth = tensor.shape
        width = sketch_one.shape[2]
        fits = (
            gx > 1
            and gy % gx == 0
            and depth % gx == 0
            and width % BLOCK == 0
            and rows_two % (8 * gx) == 0
            and rows_one % (8 * gy) == 0
            and width % (8 * gy) == 0
        )
        if fits:
            return local_kernels(gx, gy, tensor, sketch_one, sketch_two)
        return local_plain(tensor, sketch_one, sketch_two)

    in_specs = (P("gx", "gy", None), P("gy", None, None), P("gx", None, None))
    out_specs = (P("gx", None), P("gy", None), P("gx", "gy", None))
    return jax.shard_map(local, mesh=mesh, in_specs=in_specs, out_specs=out_specs, check_vma=False)
```

```python
import functools

import jax
import jax.numpy as jnp
from jax import lax
from jax.experimental import pallas as pl
from jax.experimental.pallas import tpu as pltpu
from jax.sharding import PartitionSpec as P

HIGHEST = lax.Precision.HIGHEST
MESH = pl.DeviceIdType.MESH
BLOCK = 64
VMEM_BYTES = 56 * 1024 * 1024


def gram_local(matrix):
    return jnp.dot(matrix.T, matrix, precision=HIGHEST)


def apply_factor(gram_total, matrix):
    factor = jnp.linalg.cholesky(gram_total)
    return lax.linalg.triangular_solve(
        factor, matrix, left_side=False, lower=True, transpose_a=True
    )


def local_plain(tensor, sketch_one, sketch_two):
    rows_one, rows_two, depth = tensor.shape
    width = sketch_one.shape[2]
    unfolded = tensor.reshape(rows_one, rows_two * depth)
    partial_sketch = jnp.dot(
        unfolded, sketch_one.reshape(rows_two * depth, width), precision=HIGHEST
    )
    first_sketch = lax.psum(partial_sketch, "gy")
    gram_total = lax.psum(gram_local(first_sketch), "gx")
    basis_one = apply_factor(gram_total, first_sketch)
    rank_rows = width // lax.axis_size("gx")
    partial_core = lax.psum_scatter(
        lax.dot_general(basis_one, unfolded, (((0,), (0,)), ((), ())), precision=HIGHEST),
        "gx",
        scatter_dimension=0,
        tiled=True,
    )
    partial_core = partial_core.reshape(rank_rows, rows_two, depth)
    second_part = jnp.einsum("rjk,rkc->jc", partial_core, sketch_two, precision=HIGHEST)
    second_sketch = lax.psum(second_part, "gx")
    gram_second = lax.psum(gram_local(second_sketch), "gy")
    basis_two = apply_factor(gram_second, second_sketch)
    core_terms = jnp.einsum("rjk,js->rsk", partial_core, basis_two, precision=HIGHEST)
    core = lax.psum_scatter(core_terms, "gy", scatter_dimension=1, tiled=True)
    return (basis_one, basis_two, core)


def nn(a, b):
    return jnp.dot(a, b, precision=HIGHEST, preferred_element_type=jnp.float32)


def nt(a, b):
    return lax.dot_general(
        a, b, (((1,), (1,)), ((), ())), precision=HIGHEST, preferred_element_type=jnp.float32
    )


def tn(a, b):
    return lax.dot_general(
        a, b, (((0,), (0,)), ((), ())), precision=HIGHEST, preferred_element_type=jnp.float32
    )


def eliminate(square):
    b = square.shape[0]
    eye = (
        lax.broadcasted_iota(jnp.int32, (b, b), 0) == lax.broadcasted_iota(jnp.int32, (b, b), 1)
    ).astype(jnp.float32)
    full = jnp.concatenate([square, eye], axis=1)
    lanes = 2 * b
    groups = [full[g * 8 : g * 8 + 8] for g in range(b // 8)]
    sub = lax.broadcasted_iota(jnp.int32, (8, lanes), 0)
    for g in range(b // 8):
        later = range(g, b // 8)
        cols = []
        for j in range(8):
            lane = g * 8 + j
            cols.append(
                {h: jnp.broadcast_to(groups[h][:, lane : lane + 1], (8, lanes)) for h in later}
            )
        panel = groups[g]
        scale = jnp.zeros((8, lanes), jnp.float32)
        scaled_rows = []
        for j in range(8):
            col = cols[j]
            head = col[g]
            pivot = jnp.broadcast_to(head[j : j + 1], (8, lanes))
            inverse = 1.0 / pivot
            scale = jnp.where(sub == j, pivot, scale)
            below = jnp.where(sub > j, head, 0.0)
            row = jnp.broadcast_to(panel[j : j + 1], (8, lanes)) * inverse
            scaled_rows.append(row)
            for l in range(j + 1, 8):
                factor = jnp.broadcast_to(head[l : l + 1], (8, lanes)) * inverse
                for h in later:
                    cols[l][h] = cols[l][h] - (below if h == g else col[h]) * factor
            panel = panel - below * row
        for h in later:
            if h > g:
                value = groups[h]
                for j in range(8):
                    value = value - cols[j][h] * scaled_rows[j]
                groups[h] = value
        groups[g] = panel * lax.rsqrt(scale)
    return jnp.concatenate(groups, axis=0)[:, b:]


def factor_inverse(gram, work):
    n = gram.shape[0]
    work[:, :n] = gram
    work[:, n : 2 * n] = (
        lax.broadcasted_iota(jnp.int32, (n, n), 0) == lax.broadcasted_iota(jnp.int32, (n, n), 1)
    ).astype(jnp.float32)
    for start in range(0, n, BLOCK):
        stop = start + BLOCK
        inv = eliminate(work[start:stop, start:stop])
        rows = nn(inv, work[start:stop, :])
        if stop < n:
            panel = nt(work[stop:n, start:stop], inv)
            work[stop:n, :] = work[stop:n, :] - nn(panel, rows)
        work[start:stop, n:] = rows[:, n:]


def start_copy(source, target, send_sem, recv_sem, axis, peer):
    copy = pltpu.make_async_remote_copy(
        src_ref=source,
        dst_ref=target,
        send_sem=send_sem,
        recv_sem=recv_sem,
        device_id={axis: peer},
        device_id_type=MESH,
    )
    copy.start()
    return copy


def scatter_start(source, slots, send, recv, axis, size, chunk):
    me = lax.axis_index(axis)
    copies = []
    for d in range(1, size):
        peer = lax.rem(me + d, size)
        copies.append(
            start_copy(
                chunk(source, peer), slots.at[d - 1], send.at[d - 1], recv.at[d - 1], axis, peer
            )
        )
    return copies


def gather_start(target, send, recv, axis, size, chunk):
    me = lax.axis_index(axis)
    copies = []
    for d in range(1, size):
        peer = lax.rem(me + d, size)
        mine = chunk(target, me)
        copies.append(start_copy(mine, mine, send.at[d - 1], recv.at[d - 1], axis, peer))
    return copies


def finish(copies):
    for copy in copies:
        copy.wait()


def row_chunk(rows):
    def chunk(ref, index):
        return ref.at[pl.ds(pl.multiple_of(index * rows, rows), rows)]

    return chunk


def lead_chunk(ref, index):
    return ref.at[index]


def barrier_all(gx, gy):
    a, b = lax.axis_index("gx"), lax.axis_index("gy")
    ratio = gy // gx
    barrier = pltpu.get_barrier_semaphore()
    for axis, size, me in (("gx", gx, a), ("gy", gy, b)):
        for d in range(1, size):
            pl.semaphore_signal(
                barrier, inc=1, device_id={axis: lax.rem(me + d, size)}, device_id_type=MESH
            )
    for sa in range(gx):
        for sb in range(ratio):
            @pl.when(jnp.logical_not(jnp.logical_and(sa == a, a * ratio + sb == b)))
            def _():
                pl.semaphore_signal(
                    barrier, inc=1, device_id={"gx": sa, "gy": a * ratio + sb}, device_id_type=MESH
                )
    pl.semaphore_wait(barrier, gx + gy - 2 + gy - jnp.where(b // ratio == a, 1, 0))


def sum_chunk(ref, slots, mine):
    total = ref[mine]
    for d in range(slots.shape[0]):
        total = total + slots[d]
    return total


def reduce_rows(part, out, slots, send, recv, axis, size, beside=None, after=None):
    me = lax.axis_index(axis)
    rows = part.shape[0] // size
    chunk = row_chunk(rows)
    copies = scatter_start(part, slots, send.at[0], recv.at[0], axis, size, chunk)
    if beside is not None:
        beside()
    finish(copies)
    mine = pl.ds(pl.multiple_of(me * rows, rows), rows)
    out[mine, :] = sum_chunk(part, slots, mine)
    copies = gather_start(out, send.at[1], recv.at[1], axis, size, chunk)
    if after is not None:
        after()
    finish(copies)


def exchange_pieces(gx, gy, pieces, got, out_ref, send, recv):
    a, b = lax.axis_index("gx"), lax.axis_index("gy")
    ratio = gy // gx
    inside = b // ratio == a
    slot = a * ratio + lax.rem(b, ratio)

    def outgoing(g):
        return pltpu.make_async_remote_copy(
            src_ref=pieces.at[g],
            dst_ref=got.at[slot],
            send_sem=send.at[g],
            recv_sem=recv.at[slot],
            device_id={"gx": b // ratio, "gy": g},
            device_id_type=MESH,
        )

    for g in range(gy):
        @pl.when(jnp.logical_not(jnp.logical_and(inside, g == b)))
        def _():
            outgoing(g).start()

    for s in range(gx * ratio):
        own = jnp.logical_and(inside, s == slot)

        @pl.when(jnp.logical_not(own))
        def _():
            pltpu.make_async_remote_copy(
                src_ref=pieces.at[0],
                dst_ref=got.at[s],
                send_sem=send.at[0],
                recv_sem=recv.at[s],
                device_id={"gx": b // ratio, "gy": 0},
                device_id_type=MESH,
            ).wait_recv()

        @pl.when(own)
        def _():
            got[s] = pieces[b]

    per = pieces.shape[1]
    for sa in range(gx):
        for k in range(per):
            out_ref[:, sa * per + k, :] = jnp.concatenate(
                [got[sa * ratio + sb, k] for sb in range(ratio)], axis=1
            )

    for g in range(gy):
        @pl.when(jnp.logical_not(jnp.logical_and(inside, g == b)))
        def _():
            outgoing(g).wait_send()


def kernel(
    gx, gy, t_hbm, s1_hbm, s2_hbm, q1_ref, q2_ref, out_ref,
    t_ref, s1_ref, s2_ref, load, work,
    ypart, yfull, yslots, ysend, yrecv,
    gpart, gfull, gslots, gsend, grecv,
    zall, zslots, zsend, zrecv,
    s2_all, s2_got, s2send, s2recv,
    spart, sfull, sslots, ssend, srecv,
    hpart, hfull, hslots, hsend, hrecv, bsend, brecv,
    wall, wslots, wsend, wrecv,
    pieces, got, esend, erecv,
):
    depth = t_ref.shape[1]
    width = s1_ref.shape[2]
    a, b = lax.axis_index("gx"), lax.axis_index("gy")
    per = depth // gx
    loads = [
        pltpu.make_async_copy(src, dst, load.at[i])
        for i, (src, dst) in enumerate(((s1_hbm, s1_ref), (t_hbm, t_ref), (s2_hbm, s2_ref)))
    ]
    for copy in loads:
        copy.start()
    barrier_all(gx, gy)
    finish(loads)

    total = nn(t_ref[:, 0, :], s1_ref[:, 0, :])
    for k in range(1, depth):
        total = total + nn(t_ref[:, k, :], s1_ref[:, k, :])
    ypart[...] = total

    for_later = []

    def send_sketch():
        for k in range(depth):
            s2_all[k // per, k % per] = s2_ref[:, k, :]
        for_later.extend(scatter_start(s2_all, s2_got, s2send, s2recv, "gx", gx, lead_chunk))

    reduce_rows(ypart, yfull, yslots, ysend, yrecv, "gy", gy, beside=send_sketch)

    y = yfull[...]
    yt = y.T
    gpart[...] = nn(yt, y)
    z_moves = []

    def contract():
        for k in range(depth):
            zall[k // per, k % per] = nn(yt, t_ref[:, k, :])

    def send_contraction():
        z_moves.extend(scatter_start(zall, zslots, zsend, zrecv, "gx", gx, lead_chunk))

    reduce_rows(
        gpart, gfull, gslots, gsend, grecv, "gx", gx, beside=contract, after=send_contraction
    )
    factor_inverse(gfull[...], work)
    inv = work[:, width : 2 * width]
    q1_ref[...] = nt(yfull[...], inv)
    finish(z_moves)
    z = sum_chunk(zall, zslots, a)
    p = [nn(inv, z[k]) for k in range(per)]

    finish(for_later)
    ranks = s2_all.shape[2]
    s2_got_all = s2_all.at[a]
    total = None
    for d in range(gx):
        origin = lax.rem(a + gx - d, gx)
        for k in range(per):
            block = s2_got_all[k] if d == 0 else s2_got[d - 1, k]
            work[pl.ds(pl.multiple_of(origin * ranks, ranks), ranks), k * width : (k + 1) * width] = (
                block
            )
    for k in range(per):
        term = tn(p[k], work[:, k * width : (k + 1) * width])
        total = term if total is None else total + term
    spart[...] = total
    reduce_rows(spart, sfull, sslots, ssend, srecv, "gx", gx)

    sketch = sfull[...]
    hpart[...] = tn(sketch, sketch)
    part = wall.shape[2]
    w_moves = []

    def contract_second():
        for k in range(per):
            w = nn(p[k], sketch)
            for g in range(gy):
                wall[g, k] = w[g * part : (g + 1) * part]

    def send_second():
        w_moves.extend(scatter_start(wall, wslots, wsend, wrecv, "gy", gy, lead_chunk))

    band = width // gx
    strip = band // gy

    def strip_chunk(ref, index):
        return ref.at[pl.ds(pl.multiple_of(a * band + index * strip, strip), strip)]

    copies = scatter_start(hpart, hslots, hsend.at[0], hrecv.at[0], "gy", gy, strip_chunk)
    contract_second()
    finish(copies)
    mine = pl.ds(pl.multiple_of(a * band + b * strip, strip), strip)
    hfull[mine, :] = sum_chunk(hpart, hslots, mine)
    copies = gather_start(hfull, hsend.at[1], hrecv.at[1], "gy", gy, strip_chunk)
    send_second()
    finish(copies)
    finish(gather_start(hfull, bsend, brecv, "gx", gx, row_chunk(band)))
    factor_inverse(hfull[...], work)
    q2_ref[...] = nt(sfull[...], work[:, width:])
    finish(w_moves)
    w = sum_chunk(wall, wslots, b)
    inv = work[:, width : 2 * width]
    for k in range(per):
        turned = nt(inv, w[k])
        for g in range(gy):
            pieces[g, k] = turned[g * part : (g + 1) * part]
    exchange_pieces(gx, gy, pieces, got, out_ref, esend, erecv)


def local_kernels(gx, gy, tensor, sketch_one, sketch_two):
    rows_one, rows_two, depth = tensor.shape
    width = sketch_one.shape[2]
    per = depth // gx
    ranks = sketch_two.shape[0]
    part = width // gy
    f32 = jnp.float32
    V = lambda *shape: pltpu.VMEM(shape, f32)
    D = lambda *shape: pltpu.SemaphoreType.DMA(shape)

    def sums(rows, size):
        return [
            V(rows, width), V(rows, width), V(size - 1, rows // size, width),
            D(2, size - 1), D(2, size - 1),
        ]

    turned = jnp.swapaxes(tensor, 1, 2)
    vmem = pl.BlockSpec(memory_space=pltpu.VMEM)
    basis_one, basis_two, core = pl.pallas_call(
        functools.partial(kernel, gx, gy),
        out_shape=[
            jax.ShapeDtypeStruct((rows_one, width), f32),
            jax.ShapeDtypeStruct((rows_two, width), f32),
            jax.ShapeDtypeStruct((part, depth, ranks), f32),
        ],
        in_specs=[pl.BlockSpec(memory_space=pl.ANY)] * 3,
        out_specs=[vmem] * 3,
        scratch_shapes=[
            V(*turned.shape), V(*sketch_one.shape), V(*sketch_two.shape), D(3),
            V(width, max(2, per) * width),
            *sums(rows_one, gy),
            *sums(width, gx),
            V(gx, per, width, rows_two), V(gx - 1, per, width, rows_two), D(gx - 1), D(gx - 1),
            V(gx, per, ranks, width), V(gx - 1, per, ranks, width), D(gx - 1), D(gx - 1),
            *sums(rows_two, gx),
            V(width, width), V(width, width), V(gy - 1, width // (gx * gy), width),
            D(2, gy - 1), D(2, gy - 1), D(gx - 1), D(gx - 1),
            V(gy, per, part, width), V(gy - 1, per, part, width), D(gy - 1), D(gy - 1),
            V(gy, per, part, part), V(gy, per, part, part), D(gy), D(gy),
        ],
        compiler_params=pltpu.CompilerParams(
            vmem_limit_bytes=VMEM_BYTES, collective_id=1, has_side_effects=True
        ),
    )(turned, sketch_one, sketch_two)
    return basis_one, basis_two, jnp.transpose(core, (2, 0, 1))


def solution(mesh):
    gx, gy = mesh.shape["gx"], mesh.shape["gy"]

    def local(tensor, sketch_one, sketch_two):
        rows_one, rows_two, depth = tensor.shape
        width = sketch_one.shape[2]
        fits = (
            gx > 1
            and gy % gx == 0
            and depth % gx == 0
            and width % BLOCK == 0
            and rows_two % (8 * gx) == 0
            and rows_one % (8 * gy) == 0
            and width % (8 * gy * gx) == 0
        )
        if fits:
            return local_kernels(gx, gy, tensor, sketch_one, sketch_two)
        return local_plain(tensor, sketch_one, sketch_two)

    in_specs = (P("gx", "gy", None), P("gy", None, None), P("gx", None, None))
    out_specs = (P("gx", None), P("gy", None), P("gx", "gy", None))
    return jax.shard_map(local, mesh=mesh, in_specs=in_specs, out_specs=out_specs, check_vma=False)
```

```python
import functools

import jax
import jax.numpy as jnp
from jax import lax
from jax.experimental import pallas as pl
from jax.experimental.pallas import tpu as pltpu
from jax.sharding import PartitionSpec as P

HIGHEST = lax.Precision.HIGHEST
MESH = pl.DeviceIdType.MESH
BLOCK = 64
VMEM_BYTES = 56 * 1024 * 1024


def gram_local(matrix):
    return jnp.dot(matrix.T, matrix, precision=HIGHEST)


def apply_factor(gram_total, matrix):
    factor = jnp.linalg.cholesky(gram_total)
    return lax.linalg.triangular_solve(
        factor, matrix, left_side=False, lower=True, transpose_a=True
    )


def local_plain(tensor, sketch_one, sketch_two):
    rows_one, rows_two, depth = tensor.shape
    width = sketch_one.shape[2]
    unfolded = tensor.reshape(rows_one, rows_two * depth)
    partial_sketch = jnp.dot(
        unfolded, sketch_one.reshape(rows_two * depth, width), precision=HIGHEST
    )
    first_sketch = lax.psum(partial_sketch, "gy")
    gram_total = lax.psum(gram_local(first_sketch), "gx")
    basis_one = apply_factor(gram_total, first_sketch)
    rank_rows = width // lax.axis_size("gx")
    partial_core = lax.psum_scatter(
        lax.dot_general(basis_one, unfolded, (((0,), (0,)), ((), ())), precision=HIGHEST),
        "gx",
        scatter_dimension=0,
        tiled=True,
    )
    partial_core = partial_core.reshape(rank_rows, rows_two, depth)
    second_part = jnp.einsum("rjk,rkc->jc", partial_core, sketch_two, precision=HIGHEST)
    second_sketch = lax.psum(second_part, "gx")
    gram_second = lax.psum(gram_local(second_sketch), "gy")
    basis_two = apply_factor(gram_second, second_sketch)
    core_terms = jnp.einsum("rjk,js->rsk", partial_core, basis_two, precision=HIGHEST)
    core = lax.psum_scatter(core_terms, "gy", scatter_dimension=1, tiled=True)
    return (basis_one, basis_two, core)


def nn(a, b):
    return jnp.dot(a, b, precision=HIGHEST, preferred_element_type=jnp.float32)


def nt(a, b):
    return lax.dot_general(
        a, b, (((1,), (1,)), ((), ())), precision=HIGHEST, preferred_element_type=jnp.float32
    )


def tn(a, b):
    return lax.dot_general(
        a, b, (((0,), (0,)), ((), ())), precision=HIGHEST, preferred_element_type=jnp.float32
    )


def eliminate(square):
    b = square.shape[0]
    eye = (
        lax.broadcasted_iota(jnp.int32, (b, b), 0) == lax.broadcasted_iota(jnp.int32, (b, b), 1)
    ).astype(jnp.float32)
    full = jnp.concatenate([square, eye], axis=1)
    lanes = 2 * b
    groups = [full[g * 8 : g * 8 + 8] for g in range(b // 8)]
    sub = lax.broadcasted_iota(jnp.int32, (8, lanes), 0)
    for g in range(b // 8):
        later = range(g, b // 8)
        cols = []
        for j in range(8):
            lane = g * 8 + j
            cols.append(
                {h: jnp.broadcast_to(groups[h][:, lane : lane + 1], (8, lanes)) for h in later}
            )
        panel = groups[g]
        scale = jnp.zeros((8, lanes), jnp.float32)
        scaled_rows = []
        for j in range(8):
            col = cols[j]
            head = col[g]
            pivot = jnp.broadcast_to(head[j : j + 1], (8, lanes))
            inverse = 1.0 / pivot
            scale = jnp.where(sub == j, pivot, scale)
            below = jnp.where(sub > j, head, 0.0)
            row = jnp.broadcast_to(panel[j : j + 1], (8, lanes)) * inverse
            scaled_rows.append(row)
            for l in range(j + 1, 8):
                factor = jnp.broadcast_to(head[l : l + 1], (8, lanes)) * inverse
                for h in later:
                    cols[l][h] = cols[l][h] - (below if h == g else col[h]) * factor
            panel = panel - below * row
        for h in later:
            if h > g:
                value = groups[h]
                for j in range(8):
                    value = value - cols[j][h] * scaled_rows[j]
                groups[h] = value
        groups[g] = panel * lax.rsqrt(scale)
    return jnp.concatenate(groups, axis=0)[:, b:]


def factor_inverse(gram, work):
    n = gram.shape[0]
    work[:, :n] = gram
    work[:, n : 2 * n] = (
        lax.broadcasted_iota(jnp.int32, (n, n), 0) == lax.broadcasted_iota(jnp.int32, (n, n), 1)
    ).astype(jnp.float32)
    for start in range(0, n, BLOCK):
        stop = start + BLOCK
        inv = eliminate(work[start:stop, start:stop])
        rows = nn(inv, work[start:stop, :])
        if stop < n:
            panel = nt(work[stop:n, start:stop], inv)
            work[stop:n, :] = work[stop:n, :] - nn(panel, rows)
        work[start:stop, n:] = rows[:, n:]


def start_copy(source, target, send_sem, recv_sem, axis, peer):
    copy = pltpu.make_async_remote_copy(
        src_ref=source,
        dst_ref=target,
        send_sem=send_sem,
        recv_sem=recv_sem,
        device_id={axis: peer},
        device_id_type=MESH,
    )
    copy.start()
    return copy


def scatter_start(source, slots, send, recv, axis, size, chunk):
    me = lax.axis_index(axis)
    copies = []
    for d in range(1, size):
        peer = lax.rem(me + d, size)
        copies.append(
            start_copy(
                chunk(source, peer), slots.at[d - 1], send.at[d - 1], recv.at[d - 1], axis, peer
            )
        )
    return copies


def gather_start(target, send, recv, axis, size, chunk):
    me = lax.axis_index(axis)
    copies = []
    for d in range(1, size):
        peer = lax.rem(me + d, size)
        mine = chunk(target, me)
        copies.append(start_copy(mine, mine, send.at[d - 1], recv.at[d - 1], axis, peer))
    return copies


def finish(copies):
    for copy in copies:
        copy.wait()


def row_chunk(rows):
    def chunk(ref, index):
        return ref.at[pl.ds(pl.multiple_of(index * rows, rows), rows)]

    return chunk


def lead_chunk(ref, index):
    return ref.at[index]


def barrier_all(gx, gy):
    a, b = lax.axis_index("gx"), lax.axis_index("gy")
    ratio = gy // gx
    barrier = pltpu.get_barrier_semaphore()
    for axis, size, me in (("gx", gx, a), ("gy", gy, b)):
        for d in range(1, size):
            pl.semaphore_signal(
                barrier, inc=1, device_id={axis: lax.rem(me + d, size)}, device_id_type=MESH
            )
    for sa in range(gx):
        for sb in range(ratio):
            @pl.when(jnp.logical_not(jnp.logical_and(sa == a, a * ratio + sb == b)))
            def _():
                pl.semaphore_signal(
                    barrier, inc=1, device_id={"gx": sa, "gy": a * ratio + sb}, device_id_type=MESH
                )
    pl.semaphore_wait(barrier, gx + gy - 2 + gy - jnp.where(b // ratio == a, 1, 0))


def sum_chunk(ref, slots, mine):
    total = ref[mine]
    for d in range(slots.shape[0]):
        total = total + slots[d]
    return total


def reduce_rows(part, out, slots, send, recv, axis, size, beside=None, after=None):
    me = lax.axis_index(axis)
    rows = part.shape[0] // size
    chunk = row_chunk(rows)
    copies = scatter_start(part, slots, send.at[0], recv.at[0], axis, size, chunk)
    if beside is not None:
        beside()
    finish(copies)
    mine = pl.ds(pl.multiple_of(me * rows, rows), rows)
    out[mine, :] = sum_chunk(part, slots, mine)
    copies = gather_start(out, send.at[1], recv.at[1], axis, size, chunk)
    if after is not None:
        after()
    finish(copies)


def pair_start(blocks, slots, send, recv, axis):
    me = lax.axis_index(axis)
    other = 1 - lax.rem(me, 2)
    return start_copy(
        blocks.at[other], slots, send, recv, axis, (me // 2) * 2 + other
    )


def across_start(blocks, slots, middle, target, send, recv, axis, size):
    me = lax.axis_index(axis)
    inner, outer = lax.rem(me, 2), me // 2
    middle[...] = blocks[inner] + slots[...]
    copies = []
    for d in range(1, size // 2):
        peer = lax.rem(outer + d, size // 2)
        copies.append(
            start_copy(
                middle.at[peer], target.at[d - 1], send.at[d - 1], recv.at[d - 1], axis,
                peer * 2 + inner,
            )
        )
    return copies


def exchange_pieces(gx, gy, pieces, got, out_ref, send, recv):
    a, b = lax.axis_index("gx"), lax.axis_index("gy")
    ratio = gy // gx
    inside = b // ratio == a
    slot = a * ratio + lax.rem(b, ratio)

    def outgoing(g):
        return pltpu.make_async_remote_copy(
            src_ref=pieces.at[g],
            dst_ref=got.at[slot],
            send_sem=send.at[g],
            recv_sem=recv.at[slot],
            device_id={"gx": b // ratio, "gy": g},
            device_id_type=MESH,
        )

    for g in range(gy):
        @pl.when(jnp.logical_not(jnp.logical_and(inside, g == b)))
        def _():
            outgoing(g).start()

    for s in range(gx * ratio):
        own = jnp.logical_and(inside, s == slot)

        @pl.when(jnp.logical_not(own))
        def _():
            pltpu.make_async_remote_copy(
                src_ref=pieces.at[0],
                dst_ref=got.at[s],
                send_sem=send.at[0],
                recv_sem=recv.at[s],
                device_id={"gx": b // ratio, "gy": 0},
                device_id_type=MESH,
            ).wait_recv()

        @pl.when(own)
        def _():
            got[s] = pieces[b]

    per = pieces.shape[1]
    for sa in range(gx):
        for k in range(per):
            out_ref[:, sa * per + k, :] = jnp.concatenate(
                [got[sa * ratio + sb, k] for sb in range(ratio)], axis=1
            )

    for g in range(gy):
        @pl.when(jnp.logical_not(jnp.logical_and(inside, g == b)))
        def _():
            outgoing(g).wait_send()


def kernel(
    gx, gy, t_hbm, s1_hbm, s2_hbm, q1_ref, q2_ref, out_ref,
    t_ref, s1_ref, s2_ref, load, work,
    ypart, yfull, yslots, ysend, yrecv,
    gpart, gfull, gslots, gsend, grecv,
    zall, zpair, zmid, zslots, zsend, zrecv,
    s2_all, s2_got, s2send, s2recv,
    spart, sfull, sslots, ssend, srecv,
    hpart, hfull, hslots, hsend, hrecv, bsend, brecv,
    wall, wpair, wmid, wslots, wsend, wrecv,
    pieces, got, esend, erecv,
):
    depth = t_ref.shape[1]
    width = s1_ref.shape[2]
    a, b = lax.axis_index("gx"), lax.axis_index("gy")
    per = depth // gx
    loads = [
        pltpu.make_async_copy(src, dst, load.at[i])
        for i, (src, dst) in enumerate(((s1_hbm, s1_ref), (t_hbm, t_ref), (s2_hbm, s2_ref)))
    ]
    for copy in loads:
        copy.start()
    barrier_all(gx, gy)
    finish(loads)

    total = nn(t_ref[:, 0, :], s1_ref[:, 0, :])
    for k in range(1, depth):
        total = total + nn(t_ref[:, k, :], s1_ref[:, k, :])
    ypart[...] = total

    for_later = []

    def send_sketch():
        for k in range(depth):
            s2_all[k // per, k % per] = s2_ref[:, k, :]
        for_later.extend(scatter_start(s2_all, s2_got, s2send, s2recv, "gx", gx, lead_chunk))

    reduce_rows(ypart, yfull, yslots, ysend, yrecv, "gy", gy, beside=send_sketch)

    y = yfull[...]
    yt = y.T
    gpart[...] = nn(yt, y)
    z_moves = []

    def contract():
        for k in range(depth):
            zall[(k // per) % 2, k // per // 2, k % per] = nn(yt, t_ref[:, k, :])

    def send_contraction():
        z_moves.append(pair_start(zall, zpair, zsend.at[gx // 2 - 1], zrecv.at[gx // 2 - 1], "gx"))

    reduce_rows(
        gpart, gfull, gslots, gsend, grecv, "gx", gx, beside=contract, after=send_contraction
    )
    finish(z_moves)
    z_moves = across_start(zall, zpair, zmid, zslots, zsend, zrecv, "gx", gx)
    factor_inverse(gfull[...], work)
    inv = work[:, width : 2 * width]
    q1_ref[...] = nt(yfull[...], inv)
    finish(z_moves)
    z = sum_chunk(zmid, zslots, a // 2)
    p = [nn(inv, z[k]) for k in range(per)]

    finish(for_later)
    ranks = s2_all.shape[2]
    s2_got_all = s2_all.at[a]
    total = None
    for d in range(gx):
        origin = lax.rem(a + gx - d, gx)
        for k in range(per):
            block = s2_got_all[k] if d == 0 else s2_got[d - 1, k]
            work[pl.ds(pl.multiple_of(origin * ranks, ranks), ranks), k * width : (k + 1) * width] = (
                block
            )
    for k in range(per):
        term = tn(p[k], work[:, k * width : (k + 1) * width])
        total = term if total is None else total + term
    spart[...] = total
    reduce_rows(spart, sfull, sslots, ssend, srecv, "gx", gx)

    sketch = sfull[...]
    hpart[...] = tn(sketch, sketch)
    part = wall.shape[3]
    w_moves = []

    def contract_second():
        for k in range(per):
            w = nn(p[k], sketch)
            for g in range(gy):
                wall[g % 2, g // 2, k] = w[g * part : (g + 1) * part]

    def send_second():
        w_moves.append(pair_start(wall, wpair, wsend.at[gy // 2 - 1], wrecv.at[gy // 2 - 1], "gy"))

    band = width // gx
    strip = band // gy

    def strip_chunk(ref, index):
        return ref.at[pl.ds(pl.multiple_of(a * band + index * strip, strip), strip)]

    copies = scatter_start(hpart, hslots, hsend.at[0], hrecv.at[0], "gy", gy, strip_chunk)
    contract_second()
    finish(copies)
    mine = pl.ds(pl.multiple_of(a * band + b * strip, strip), strip)
    hfull[mine, :] = sum_chunk(hpart, hslots, mine)
    copies = gather_start(hfull, hsend.at[1], hrecv.at[1], "gy", gy, strip_chunk)
    send_second()
    finish(copies)
    finish(gather_start(hfull, bsend, brecv, "gx", gx, row_chunk(band)))
    finish(w_moves)
    w_moves = across_start(wall, wpair, wmid, wslots, wsend, wrecv, "gy", gy)
    factor_inverse(hfull[...], work)
    q2_ref[...] = nt(sfull[...], work[:, width:])
    finish(w_moves)
    w = sum_chunk(wmid, wslots, b // 2)
    inv = work[:, width : 2 * width]
    for k in range(per):
        turned = nt(inv, w[k])
        for g in range(gy):
            pieces[g, k] = turned[g * part : (g + 1) * part]
    exchange_pieces(gx, gy, pieces, got, out_ref, esend, erecv)


def local_kernels(gx, gy, tensor, sketch_one, sketch_two):
    rows_one, rows_two, depth = tensor.shape
    width = sketch_one.shape[2]
    per = depth // gx
    ranks = sketch_two.shape[0]
    part = width // gy
    f32 = jnp.float32
    V = lambda *shape: pltpu.VMEM(shape, f32)
    D = lambda *shape: pltpu.SemaphoreType.DMA(shape)

    def sums(rows, size):
        return [
            V(rows, width), V(rows, width), V(size - 1, rows // size, width),
            D(2, size - 1), D(2, size - 1),
        ]

    turned = jnp.swapaxes(tensor, 1, 2)
    vmem = pl.BlockSpec(memory_space=pltpu.VMEM)
    basis_one, basis_two, core = pl.pallas_call(
        functools.partial(kernel, gx, gy),
        out_shape=[
            jax.ShapeDtypeStruct((rows_one, width), f32),
            jax.ShapeDtypeStruct((rows_two, width), f32),
            jax.ShapeDtypeStruct((part, depth, ranks), f32),
        ],
        in_specs=[pl.BlockSpec(memory_space=pl.ANY)] * 3,
        out_specs=[vmem] * 3,
        scratch_shapes=[
            V(*turned.shape), V(*sketch_one.shape), V(*sketch_two.shape), D(3),
            V(width, max(2, per) * width),
            *sums(rows_one, gy),
            *sums(width, gx),
            V(2, gx // 2, per, width, rows_two), V(gx // 2, per, width, rows_two),
            V(gx // 2, per, width, rows_two), V(gx // 2 - 1, per, width, rows_two),
            D(gx // 2), D(gx // 2),
            V(gx, per, ranks, width), V(gx - 1, per, ranks, width), D(gx - 1), D(gx - 1),
            *sums(rows_two, gx),
            V(width, width), V(width, width), V(gy - 1, width // (gx * gy), width),
            D(2, gy - 1), D(2, gy - 1), D(gx - 1), D(gx - 1),
            V(2, gy // 2, per, part, width), V(gy // 2, per, part, width),
            V(gy // 2, per, part, width), V(gy // 2 - 1, per, part, width),
            D(gy // 2), D(gy // 2),
            V(gy, per, part, part), V(gy, per, part, part), D(gy), D(gy),
        ],
        compiler_params=pltpu.CompilerParams(
            vmem_limit_bytes=VMEM_BYTES, collective_id=1, has_side_effects=True
        ),
    )(turned, sketch_one, sketch_two)
    return basis_one, basis_two, jnp.transpose(core, (2, 0, 1))


def solution(mesh):
    gx, gy = mesh.shape["gx"], mesh.shape["gy"]

    def local(tensor, sketch_one, sketch_two):
        rows_one, rows_two, depth = tensor.shape
        width = sketch_one.shape[2]
        fits = (
            gx > 2
            and gx % 2 == 0
            and gy % gx == 0
            and depth % gx == 0
            and width % BLOCK == 0
            and rows_two % (8 * gx) == 0
            and rows_one % (8 * gy) == 0
            and width % (8 * gy * gx) == 0
        )
        if fits:
            return local_kernels(gx, gy, tensor, sketch_one, sketch_two)
        return local_plain(tensor, sketch_one, sketch_two)

    in_specs = (P("gx", "gy", None), P("gy", None, None), P("gx", None, None))
    out_specs = (P("gx", None), P("gy", None), P("gx", "gy", None))
    return jax.shard_map(local, mesh=mesh, in_specs=in_specs, out_specs=out_specs, check_vma=False)
```
